128 devices in a mesh: fsdp: 16 (over x_hi, z, core), tensor: 8 (over y, x_lo).
Axes of the slice: x: 4 (x_hi: 2, x_lo: 2; x = x_hi * 2 + x_lo), y: 4, z: 4, core: 2. Of those that a mesh axis runs over, the one named last changes fastest.
Arguments:
- grad: bfloat16 [12288, 53248], P('fsdp', 'tensor'), may hold values from -2 to 2
- old_stats: float32 [12288, 3, 768], P(('fsdp', 'tensor')), may hold values from -6 to 6
Outputs:
- new_stats: float32 [12288, 3, 768], P(('fsdp', 'tensor'))
The draws below stay inside these ranges and needn't reach their ends.
All inputs are finite; a program needn't handle non-finite values.
Results may differ from the reference program's by a relative error of at most 0.0003.
Values may be sent and summed in bfloat16 or wider, within the bound.
No kernel may reach another device: no remote copies, remote signals or barrier semaphores. Data moves between devices by JAX's collectives and lax.ppermute only.
A program may use at most 128 MiB of HBM per device.

```python
import jax
import jax.numpy as jnp
from jax import lax

COLS = 53248
BLK = 768
ROWS = 12288
N_FSDP = 16


def draw_grad(key, part):
    key = jax.random.fold_in(key, 11)
    value_key = jax.random.fold_in(key, 0)
    values = 0.3 * jax.random.normal(value_key, (ROWS, COLS), jnp.float32)
    return jnp.clip(values, -1.8, 1.8).astype(jnp.bfloat16)


def block_levels(key, dims, pieces, low, largest):
    gain = 1.0
    for axis_at, parts in pieces:
        draws = jax.random.uniform(jax.random.fold_in(jax.random.fold_in(key, 6), axis_at), (parts,), jnp.float32, low / len(pieces), largest / len(pieces))
        gain = gain * jnp.repeat(jnp.exp(draws), dims[axis_at] // parts).reshape((-1,) + (1,) * (len(dims) - 1 - axis_at))
    return gain


def noise(key, extent, spread, most, cuts=(), kind=jnp.bfloat16):
    array = spread * jax.random.normal(key, extent, jnp.float32)
    if cuts:
        array = array * block_levels(key, extent, cuts, -0.22, 0.18)
    return jnp.clip(array, -most, most).astype(kind)


def setup_inputs(seed: int = 0) -> dict:
    keys = jax.random.split(jax.random.key(seed), 3)
    grad = draw_grad(jax.random.fold_in(keys[2], 71), 0)
    old_stats = noise(keys[1], (ROWS, 3, BLK), 1.0, 6.0, ((0, 128),), jnp.float32)
    return dict(grad=grad, old_stats=old_stats)


decay_rate = 0.95


def reference(grad, old_stats):
    blocks = grad.reshape(N_FSDP, BLK, COLS)

    def one_block(position):
        own_rows = lax.dynamic_index_in_dim(blocks, position, 0, keepdims=False)
        products = []
        for distance in range(3):
            partner = lax.dynamic_index_in_dim(blocks, (position + distance) % N_FSDP, 0, keepdims=False)
            products.append(jnp.dot(own_rows, partner.T, preferred_element_type=jnp.float32))
        return jnp.stack(products, axis=1)

    gram = lax.map(one_block, jnp.arange(N_FSDP, dtype=jnp.int32)).reshape(ROWS, 3, BLK)
    return decay_rate * old_stats + (1.0 - decay_rate) * (COLS ** -0.5) * gram
```

```python
import functools

import jax
import jax.numpy as jnp
from jax import lax
from jax.experimental import pallas as pl
from jax.experimental.pallas import tpu as pltpu
from jax.sharding import PartitionSpec as P

COLS = 53248
decay_rate = 0.95
CHUNKS = (256, 256, 128, 128)
BEGINS = (0, 256, 512, 640)
VMEM_LIMIT = 5 << 20
AXES = ("fsdp", "tensor")


def place(x_hi, z, core, y, x_lo):
    return ((x_hi % 2) * 8 + (z % 4) * 2 + core) * 8 + (y % 4) * 2 + x_lo


def moved(value, target):
    pairs = []
    for source in range(128):
        block, shard = divmod(source, 8)
        pairs.append((source, target(block // 8, (block // 2) % 4, block % 2, shard // 2, shard % 2)))
    return lax.ppermute(value, AXES, pairs)


def next_chip(x_hi, z, core, y, x_lo, steps):
    chip = (x_hi * 4 + z + steps) % 8
    return place(chip // 4, chip % 4, core, y, x_lo)


def block_flow(x_hi, z, core, y, x_lo):
    return next_chip(x_hi, z, core, y, x_lo, 1 if core else -1)


def swap_cores(x_hi, z, core, y, x_lo):
    return place(x_hi, z, 1 - core, y, x_lo)


def swap_both(x_hi, z, core, y, x_lo):
    return place(x_hi, z, 1 - core, y, 1 - x_lo)


def to_owner(x_hi, z, core, y, x_lo):
    return next_chip(x_hi, z, core, y, x_lo, -1 if core else 0)


def to_owner_x(x_hi, z, core, y, x_lo):
    return next_chip(x_hi, z, core, y, 1 - x_lo, -1 if core else 0)


def swap_x(x_hi, z, core, y, x_lo):
    return place(x_hi, z, core, y, 1 - x_lo)


def along_y(steps):
    return lambda x_hi, z, core, y, x_lo: place(x_hi, z, core, y + steps, x_lo)


def contract(left, right):
    return lax.dot_general(left, right, (((1,), (1,)), ((), ())), preferred_element_type=jnp.float32)


def pick_kernel(begin, thin, where_ref, grad_ref, out_ref, sems):
    core = where_ref[0]
    copies = []
    for i in range(8):
        offset = pl.multiple_of(jnp.where(core == 0, begin + thin * i, 96 * i + begin // 8), 16)
        copies.append(pltpu.make_async_copy(grad_ref.at[pl.ds(offset, thin)], out_ref.at[pl.ds(thin * i, thin)], sems.at[i]))
    for copy in copies:
        copy.start()
    for copy in copies:
        copy.wait()


def picked(where, grad, begin, wide):
    depth = grad.shape[1]
    return pl.pallas_call(
        functools.partial(pick_kernel, begin, wide // 8),
        out_shape=jax.ShapeDtypeStruct((wide, depth), grad.dtype),
        in_specs=[pl.BlockSpec(memory_space=pltpu.SMEM), pl.BlockSpec(memory_space=pl.ANY)],
        out_specs=pl.BlockSpec(memory_space=pltpu.VMEM),
        scratch_shapes=[pltpu.SemaphoreType.DMA((8,))],
        cost_estimate=pl.CostEstimate(flops=0, bytes_accessed=4 * wide * depth, transcendentals=0),
        compiler_params=pltpu.CompilerParams(vmem_limit_bytes=VMEM_LIMIT),
    )(where, pltpu.with_memory_space_constraint(grad, pltpu.HBM))


def hold_kernel(source_ref, out_ref, sem):
    copy = pltpu.make_async_copy(source_ref, out_ref, sem)
    copy.start()
    copy.wait()


def held(value):
    return pl.pallas_call(
        hold_kernel,
        out_shape=pltpu.VMEM(value.shape, value.dtype),
        in_specs=[pl.BlockSpec(memory_space=pl.ANY)],
        out_specs=pl.BlockSpec(memory_space=pltpu.VMEM),
        scratch_shapes=[pltpu.SemaphoreType.DMA],
        cost_estimate=pl.CostEstimate(flops=0, bytes_accessed=4 * value.size, transcendentals=0),
        compiler_params=pltpu.CompilerParams(vmem_limit_bytes=VMEM_LIMIT),
    )(pltpu.with_memory_space_constraint(value, pltpu.HBM))


def resident(value):
    return pltpu.with_memory_space_constraint(value, pltpu.VMEM)


def vmem_specs(count):
    return [pl.BlockSpec(memory_space=pltpu.SMEM)] + [pl.BlockSpec(memory_space=pltpu.VMEM)] * count


def owner_rows(y, hop, side, count):
    shard = 2 * ((y + hop) & 3) + side
    return pl.ds(pl.multiple_of(count * shard, count), count)


def square_kernel(where_ref, own_ref, *refs):
    outs, total = refs[:4], refs[4]
    y = where_ref[1]
    total[...] = contract(own_ref[...], own_ref[...])
    for hop in range(4):
        for side in range(2):
            outs[hop][side] = total[owner_rows(y, hop, side, 96), :]


def squared(where, grad):
    rows, depth = grad.shape
    piece = (2, rows // 8, rows)
    return pl.pallas_call(
        square_kernel,
        out_shape=[jax.ShapeDtypeStruct(piece, jnp.float32)] * 4,
        in_specs=vmem_specs(1),
        out_specs=[pl.BlockSpec(memory_space=pltpu.VMEM)] * 4,
        scratch_shapes=[pltpu.VMEM((rows, rows), jnp.float32)],
        cost_estimate=pl.CostEstimate(
            flops=2 * rows * rows * depth, bytes_accessed=2 * depth * rows + 4 * rows * rows, transcendentals=0
        ),
        compiler_params=pltpu.CompilerParams(vmem_limit_bytes=VMEM_LIMIT),
    )(where, resident(grad))


def cross_kernel(begin, wide, where_ref, own_ref, pair_ref, got_ref, *refs):
    outs, (tall, flat, mixed) = refs[:4], refs[4:]
    core, y = where_ref[0], where_ref[1]
    thin = wide // 8
    blocks = 768 // wide

    @pl.when(core == 0)
    def _():
        tall[...] = contract(own_ref[...], got_ref[...])
        mixed[...] = contract(pair_ref[...], got_ref[...])
        for hop in range(4):
            for side in range(2):
                outs[hop][side, 0] = tall[owner_rows(y, hop, side, 96), :]

    @pl.when(core != 0)
    def _():
        flat[...] = contract(got_ref[...], own_ref[...])
        mixed[...] = contract(pair_ref[...], own_ref[begin : begin + wide, :])
        for hop in range(4):
            for side in range(2):
                rows = owner_rows(y, hop, side, thin)
                for i in range(blocks):
                    outs[hop][side, 0, i * thin : (i + 1) * thin, :] = flat[rows, i * wide : (i + 1) * wide]

    for hop in range(4):
        for side in range(2):
            outs[hop][side, 1] = mixed[owner_rows(y, hop, side, 96), :]


def crossed(where, grad, partner, arrived, begin):
    wide, depth = arrived.shape
    rows = grad.shape[0]
    piece = (2, 2, rows // 8, wide)
    return pl.pallas_call(
        functools.partial(cross_kernel, begin, wide),
        out_shape=[jax.ShapeDtypeStruct(piece, jnp.float32)] * 4,
        in_specs=vmem_specs(3),
        out_specs=[pl.BlockSpec(memory_space=pltpu.VMEM)] * 4,
        scratch_shapes=[
            pltpu.VMEM((rows, wide), jnp.float32),
            pltpu.VMEM((wide, rows), jnp.float32),
            pltpu.VMEM((rows, wide), jnp.float32),
        ],
        cost_estimate=pl.CostEstimate(
            flops=4 * rows * wide * depth, bytes_accessed=2 * depth * (2 * rows + wide) + 16 * rows * wide, transcendentals=0
        ),
        compiler_params=pltpu.CompilerParams(vmem_limit_bytes=VMEM_LIMIT),
    )(where, resident(grad), resident(partner), resident(arrived))


def total_of(refs, *at):
    return (refs[0][at] + refs[1][at]) + (refs[2][at] + refs[3][at])


def first_sums_kernel(where_ref, *refs):
    x_lo = where_ref[2]
    keep_ref, give_ref = refs[-2:]
    for side, out_ref in ((x_lo, keep_ref), (1 - x_lo, give_ref)):
        out_ref[0] = total_of(refs[:4], side)
        for j in range(len(CHUNKS) - 1):
            span = slice(BEGINS[j], BEGINS[j] + CHUNKS[j])
            for product in range(2):
                out_ref[1 + product, :, span] = total_of(refs[4 + 4 * j : 8 + 4 * j], side, product)
        for product in range(2):
            out_ref[1 + product, :, BEGINS[-1] :] = jnp.zeros((96, CHUNKS[-1]), jnp.float32)


def first_sums(where, pieces):
    shape = jax.ShapeDtypeStruct((3, 96, 768), jnp.float32)
    return pl.pallas_call(
        first_sums_kernel,
        out_shape=[shape, shape],
        in_specs=vmem_specs(len(pieces)),
        out_specs=[pl.BlockSpec(memory_space=pltpu.VMEM)] * 2,
        cost_estimate=pl.CostEstimate(flops=4 * 3 * 96 * 768 * 2, bytes_accessed=10 * 3 * 96 * 768 * 4, transcendentals=0),
        compiler_params=pltpu.CompilerParams(vmem_limit_bytes=2 * VMEM_LIMIT),
    )(where, *pieces)


def last_sums_kernel(where_ref, keep_ref, got_ref, piece_0, piece_1, piece_2, piece_3, diagonal_ref, far_ref, near_ref, give_ref):
    core, x_lo = where_ref[0], where_ref[2]
    pieces = (piece_0, piece_1, piece_2, piece_3)
    start = BEGINS[-1]
    diagonal_ref[...] = keep_ref[0] + got_ref[0]
    near_ref[:, :start] = keep_ref[2, :, :start] + got_ref[2, :, :start]
    near_ref[:, start:] = total_of(pieces, x_lo, 1)
    for product in range(2):
        give_ref[product] = total_of(pieces, 1 - x_lo, product)

    @pl.when(core == 0)
    def _():
        far_ref[:, :start] = keep_ref[1, :, :start] + got_ref[1, :, :start]
        far_ref[:, start:] = total_of(pieces, x_lo, 0)

    @pl.when(core != 0)
    def _():
        for begin, wide in zip(BEGINS, CHUNKS):
            thin = wide // 8
            for i in range(768 // wide):
                rows = slice(i * thin, (i + 1) * thin)
                if begin == start:
                    value = total_of(pieces, x_lo, 0, rows)
                else:
                    value = keep_ref[1, rows, begin : begin + wide] + got_ref[1, rows, begin : begin + wide]
                far_ref[begin // 8 : begin // 8 + thin, i * wide : (i + 1) * wide] = value


def last_sums(where, keep, got, pieces):
    shape = jax.ShapeDtypeStruct((96, 768), jnp.float32)
    return pl.pallas_call(
        last_sums_kernel,
        out_shape=[shape, shape, shape, jax.ShapeDtypeStruct((2, 96, CHUNKS[-1]), jnp.float32)],
        in_specs=vmem_specs(6),
        out_specs=[pl.BlockSpec(memory_space=pltpu.VMEM)] * 4,
        cost_estimate=pl.CostEstimate(flops=2 * 3 * 96 * 768, bytes_accessed=4 * 3 * 96 * 768 * 4, transcendentals=0),
        compiler_params=pltpu.CompilerParams(vmem_limit_bytes=VMEM_LIMIT),
    )(where, keep, got, *pieces)


def tied(*values):
    return lax.optimization_barrier(values)


def shards(grad, old_stats):
    rows = grad.shape[0]
    core = lax.axis_index("fsdp") & 1
    y, x_lo = lax.axis_index("tensor") >> 1, lax.axis_index("tensor") & 1
    where = jnp.stack([core, y, x_lo]).astype(jnp.int32)

    def spread(pieces):
        return [moved(pieces[hop], along_y(hop)) for hop in (1, 3, 2)]

    def pick(j):
        return picked(where, grad, BEGINS[j], CHUNKS[j])

    def cross(j):
        return crossed(where, here, partner, flight[j], BEGINS[j])

    partner = moved(grad, swap_cores)
    flight = [moved(pick(0), block_flow)]
    here = held(grad)
    square = squared(where, here)
    *square, partner, out1 = tied(*square, partner, pick(1))
    flight.append(moved(out1, block_flow))
    square_got = spread(square)
    partner = held(partner)
    out2, out3 = pick(2), pick(3)
    flight[0], partner, out2, out3 = tied(flight[0], partner, out2, out3)

    part0 = cross(0)
    *part0, out2, square_got[0], square_got[1], square_got[2] = tied(*part0, out2, *square_got)
    got0 = spread(part0)
    flight.append(moved(out2, block_flow))

    out3, got0[0], got0[1], got0[2] = tied(out3, *got0)
    flight.append(moved(out3, block_flow))
    flight[1], part0[0] = tied(flight[1], part0[0])
    part1 = list(cross(1))
    got1 = spread(part1)

    flight[2], part1[0] = tied(flight[2], part1[0])
    part2 = cross(2)
    *part2, got1[0], got1[1], got1[2] = tied(*part2, *got1)
    got2 = spread(part2)

    flight[3], got2[0], got2[1], got2[2] = tied(flight[3], *got2)
    firsts = [square[0], *square_got, part0[0], *got0, part1[0], *got1, part2[0], *got2]
    keep, give = first_sums(where, firsts)
    got = moved(give, swap_x)
    flight[3], keep = tied(flight[3], keep)
    part3 = cross(3)
    got3 = spread(part3)
    diagonal, far, near, give = last_sums(where, keep, got, [part3[0], *got3])

    far_more, near_more = moved(give[0], to_owner_x), moved(give[1], swap_both)
    far, near = moved(far, to_owner), moved(near, swap_cores)
    near = jnp.concatenate([near[:, :-128], near[:, -128:] + near_more], axis=1)
    far_low = jnp.pad(far_more, ((0, 0), (rows - 128, 0)))
    far_high = jnp.pad(far_more.reshape(6, 16, 128).transpose(1, 0, 2).reshape(16, rows), ((80, 0), (0, 0)))
    far = far + jnp.where(core == 0, far_low, far_high)
    summed = jnp.stack([diagonal, near, far], axis=1)
    return decay_rate * old_stats + (1.0 - decay_rate) * COLS ** (-0.5) * summed


def solution(mesh):
    return jax.shard_map(
        shards,
        mesh=mesh,
        in_specs=(P("fsdp", "tensor"), P(("fsdp", "tensor"), None, None)),
        out_specs=P(("fsdp", "tensor"), None, None),
        check_vma=False,
    )
```

```python
import functools

import jax
import jax.numpy as jnp
from jax import lax
from jax.experimental import pallas as pl
from jax.experimental.pallas import tpu as pltpu
from jax.sharding import PartitionSpec as P

COLS = 53248
decay_rate = 0.95
CHUNKS = (256, 256, 128, 128)
BEGINS = (0, 256, 512, 640)
VMEM_LIMIT = 5 << 20
SPLIT = 4608
FIRST = 2
AXES = ("fsdp", "tensor")


def place(x_hi, z, core, y, x_lo):
    return ((x_hi % 2) * 8 + (z % 4) * 2 + core) * 8 + (y % 4) * 2 + x_lo


def moved(value, target):
    pairs = []
    for source in range(128):
        block, shard = divmod(source, 8)
        pairs.append((source, target(block // 8, (block // 2) % 4, block % 2, shard // 2, shard % 2)))
    return lax.ppermute(value, AXES, pairs)


def next_chip(x_hi, z, core, y, x_lo, steps):
    chip = (x_hi * 4 + z + steps) % 8
    return place(chip // 4, chip % 4, core, y, x_lo)


def block_flow(x_hi, z, core, y, x_lo):
    return next_chip(x_hi, z, 1 - core, y, x_lo, 1 if core else -1)


def swap_cores(x_hi, z, core, y, x_lo):
    return place(x_hi, z, 1 - core, y, x_lo)


def swap_x(x_hi, z, core, y, x_lo):
    return place(x_hi, z, core, y, 1 - x_lo)


def to_owner(x_hi, z, core, y, x_lo):
    return next_chip(x_hi, z, 1 - core, y, x_lo, 0 if core else -1)


def to_owner_x(x_hi, z, core, y, x_lo):
    return to_owner(x_hi, z, core, y, 1 - x_lo)


def along_y(steps):
    return lambda x_hi, z, core, y, x_lo: place(x_hi, z, core, y + steps, x_lo)


def contract(left, right):
    return lax.dot_general(left, right, (((1,), (1,)), ((), ())), preferred_element_type=jnp.float32)


def pick_kernel(begin, thin, span, where_ref, grad_ref, out_ref, sems):
    core = where_ref[0]
    copies = []
    for i in range(8):
        offset = pl.multiple_of(jnp.where(core == 0, begin + thin * i, 96 * i + begin // 8), 16)
        source = grad_ref.at[pl.ds(offset, thin), pl.ds(span[0], span[1] - span[0])]
        copies.append(pltpu.make_async_copy(source, out_ref.at[pl.ds(thin * i, thin)], sems.at[i]))
    for copy in copies:
        copy.start()
    for copy in copies:
        copy.wait()


def picked(where, grad, begin, wide, span):
    depth = span[1] - span[0]
    return pl.pallas_call(
        functools.partial(pick_kernel, begin, wide // 8, span),
        out_shape=jax.ShapeDtypeStruct((wide, depth), grad.dtype),
        in_specs=[pl.BlockSpec(memory_space=pltpu.SMEM), pl.BlockSpec(memory_space=pl.ANY)],
        out_specs=pl.BlockSpec(memory_space=pltpu.VMEM),
        scratch_shapes=[pltpu.SemaphoreType.DMA((8,))],
        cost_estimate=pl.CostEstimate(flops=0, bytes_accessed=4 * wide * depth, transcendentals=0),
        compiler_params=pltpu.CompilerParams(vmem_limit_bytes=VMEM_LIMIT),
    )(where, pltpu.with_memory_space_constraint(grad, pltpu.HBM))


def hold_kernel(source_ref, out_ref, sem):
    copy = pltpu.make_async_copy(source_ref, out_ref, sem)
    copy.start()
    copy.wait()


def held(value):
    return pl.pallas_call(
        hold_kernel,
        out_shape=pltpu.VMEM(value.shape, value.dtype),
        in_specs=[pl.BlockSpec(memory_space=pl.ANY)],
        out_specs=pl.BlockSpec(memory_space=pltpu.VMEM),
        scratch_shapes=[pltpu.SemaphoreType.DMA],
        cost_estimate=pl.CostEstimate(flops=0, bytes_accessed=4 * value.size, transcendentals=0),
        compiler_params=pltpu.CompilerParams(vmem_limit_bytes=VMEM_LIMIT),
    )(pltpu.with_memory_space_constraint(value, pltpu.HBM))


def resident(value):
    return pltpu.with_memory_space_constraint(value, pltpu.VMEM)


def vmem_specs(count):
    return [pl.BlockSpec(memory_space=pltpu.SMEM)] + [pl.BlockSpec(memory_space=pltpu.VMEM)] * count


def owner_rows(y, hop, side, count):
    shard = 2 * ((y + hop) & 3) + side
    return pl.ds(pl.multiple_of(count * shard, count), count)


def square_kernel(where_ref, own_ref, *refs):
    outs, total = refs[:4], refs[4]
    y = where_ref[1]
    total[...] = contract(own_ref[...], own_ref[...])
    for hop in range(4):
        for side in range(2):
            outs[hop][side] = total[owner_rows(y, hop, side, 96), :]


def squared(where, grad):
    rows, depth = grad.shape
    piece = (2, rows // 8, rows)
    return pl.pallas_call(
        square_kernel,
        out_shape=[jax.ShapeDtypeStruct(piece, jnp.float32)] * 4,
        in_specs=vmem_specs(1),
        out_specs=[pl.BlockSpec(memory_space=pltpu.VMEM)] * 4,
        scratch_shapes=[pltpu.VMEM((rows, rows), jnp.float32)],
        cost_estimate=pl.CostEstimate(
            flops=2 * rows * rows * depth, bytes_accessed=2 * depth * rows + 4 * rows * rows, transcendentals=0
        ),
        compiler_params=pltpu.CompilerParams(vmem_limit_bytes=VMEM_LIMIT),
    )(where, resident(grad))


def cut_up(core, y, tall, flat, mixed, outs):
    wide = mixed.shape[1]
    thin = wide // 8

    @pl.when(core != 0)
    def _():
        for hop in range(4):
            for side in range(2):
                outs[hop][side, 0] = tall[owner_rows(y, hop, side, 96), :]

    @pl.when(core == 0)
    def _():
        for hop in range(4):
            for side in range(2):
                rows = owner_rows(y, hop, side, thin)
                for i in range(768 // wide):
                    outs[hop][side, 0, i * thin : (i + 1) * thin, :] = flat[rows, i * wide : (i + 1) * wide]

    for hop in range(4):
        for side in range(2):
            outs[hop][side, 1] = mixed[owner_rows(y, hop, side, 96), :]


def cross_kernel(begin, where_ref, own_ref, pair_ref, got_ref, *refs):
    outs, (tall, flat, mixed) = refs[:4], refs[4:]
    core = where_ref[0]
    wide = got_ref.shape[0]

    @pl.when(core == 0)
    def _():
        flat[...] = contract(got_ref[...], pair_ref[...])
        mixed[...] = contract(own_ref[...], pair_ref[begin : begin + wide, :])

    @pl.when(core != 0)
    def _():
        tall[...] = contract(pair_ref[...], got_ref[...])
        mixed[...] = contract(own_ref[...], got_ref[...])

    cut_up(core, where_ref[1], tall, flat, mixed, outs)


def early_kernel(begin, wide, where_ref, own_ref, pair_ref, mixed_ref):
    @pl.when(where_ref[0] == 0)
    def _():
        mixed_ref[...] = contract(own_ref[...], pair_ref[begin : begin + wide, :])


def middle_kernel(where_ref, own_ref, pair_ref, got_ref, tall_ref, mixed_ref):
    @pl.when(where_ref[3] != 0)
    def _():
        tall_ref[...] = contract(pair_ref[...], got_ref[...])
        mixed_ref[...] = contract(own_ref[...], got_ref[...])


def late_kernel(where_ref, own_ref, pair_ref, got_ref, early_ref, tall_ref, middle_ref, *refs):
    outs, (tall, flat, mixed) = refs[:4], refs[4:]
    core, ahead = where_ref[0], where_ref[3]

    @pl.when(core == 0)
    def _():
        flat[...] = contract(got_ref[...], pair_ref[...])
        mixed[...] = early_ref[...]

    @pl.when((core != 0) & (ahead == 0))
    def _():
        tall[...] = contract(pair_ref[...], got_ref[...])
        mixed[...] = contract(own_ref[...], got_ref[...])

    @pl.when(ahead != 0)
    def _():
        tall[...] = tall_ref[...]
        mixed[...] = middle_ref[...]

    cut_up(core, where_ref[1], tall, flat, mixed, outs)


def product_call(kernel, shapes, scratch, flops, where, *arrays):
    return pl.pallas_call(
        kernel,
        out_shape=[jax.ShapeDtypeStruct(shape, jnp.float32) for shape in shapes],
        in_specs=vmem_specs(len(arrays)),
        out_specs=[pl.BlockSpec(memory_space=pltpu.VMEM)] * len(shapes),
        scratch_shapes=[pltpu.VMEM(shape, jnp.float32) for shape in scratch],
        cost_estimate=pl.CostEstimate(flops=flops, bytes_accessed=4 * flops // 768, transcendentals=0),
        compiler_params=pltpu.CompilerParams(vmem_limit_bytes=VMEM_LIMIT),
    )(where, *[resident(array) for array in arrays])


def crossed(where, grad, partner, arrived, begin):
    wide, depth = arrived.shape
    rows = grad.shape[0]
    pieces = [(2, 2, rows // 8, wide)] * 4
    sums = [(rows, wide), (wide, rows), (rows, wide)]
    kernel = functools.partial(cross_kernel, begin)
    return product_call(kernel, pieces, sums, 4 * rows * wide * depth, where, grad, partner, arrived)


def total_of(refs, *at):
    return (refs[0][at] + refs[1][at]) + (refs[2][at] + refs[3][at])


def columns_of(product, part):
    start = 768 + product * BEGINS[FIRST] + BEGINS[part]
    return slice(start, start + CHUNKS[part])


def first_sums_kernel(where_ref, *refs):
    x_lo = where_ref[2]
    for side, out_ref in ((x_lo, refs[-2]), (1 - x_lo, refs[-1])):
        out_ref[:, :768] = total_of(refs[:4], side)
        for j in range(FIRST):
            for product in range(2):
                out_ref[:, columns_of(product, j)] = total_of(refs[4 + 4 * j : 8 + 4 * j], side, product)


def first_sums(where, pieces):
    shape = jax.ShapeDtypeStruct((96, 768 + 2 * BEGINS[FIRST]), jnp.float32)
    return pl.pallas_call(
        first_sums_kernel,
        out_shape=[shape, shape],
        in_specs=vmem_specs(len(pieces)),
        out_specs=[pl.BlockSpec(memory_space=pltpu.VMEM)] * 2,
        cost_estimate=pl.CostEstimate(flops=4 * 3 * 96 * 768 * 2, bytes_accessed=10 * 3 * 96 * 768 * 4, transcendentals=0),
        compiler_params=pltpu.CompilerParams(vmem_limit_bytes=2 * VMEM_LIMIT),
    )(where, *pieces)


def far_sums_kernel(where_ref, keep_ref, got_ref, *refs):
    pieces, (far_ref, give_ref) = refs[:-2], refs[-2:]
    core, x_lo = where_ref[0], where_ref[2]
    start = BEGINS[FIRST]
    for j in range(FIRST, len(CHUNKS)):
        columns = slice(BEGINS[j] - start, BEGINS[j] - start + CHUNKS[j])
        give_ref[:, columns] = total_of(pieces[4 * (j - FIRST) : 4 * (j - FIRST) + 4], 1 - x_lo, 0)

    @pl.when(core != 0)
    def _():
        far_ref[:, :start] = keep_ref[:, 768 : 768 + start] + got_ref[:, 768 : 768 + start]
        for j in range(FIRST, len(CHUNKS)):
            columns = slice(BEGINS[j], BEGINS[j] + CHUNKS[j])
            far_ref[:, columns] = total_of(pieces[4 * (j - FIRST) : 4 * (j - FIRST) + 4], x_lo, 0)

    @pl.when(core == 0)
    def _():
        for j, (begin, wide) in enumerate(zip(BEGINS, CHUNKS)):
            thin = wide // 8
            for i in range(768 // wide):
                rows = slice(i * thin, (i + 1) * thin)
                if j < FIRST:
                    value = keep_ref[rows, columns_of(0, j)] + got_ref[rows, columns_of(0, j)]
                else:
                    value = total_of(pieces[4 * (j - FIRST) : 4 * (j - FIRST) + 4], x_lo, 0, rows)
                far_ref[begin // 8 : begin // 8 + thin, i * wide : (i + 1) * wide] = value


def near_sums_kernel(where_ref, keep_ref, got_ref, *refs):
    pieces, (diagonal_ref, near_ref, give_ref) = refs[:-3], refs[-3:]
    x_lo = where_ref[2]
    start = BEGINS[FIRST]
    diagonal_ref[...] = keep_ref[:, :768] + got_ref[:, :768]
    near_ref[:, :start] = keep_ref[:, 768 + start :] + got_ref[:, 768 + start :]
    for j in range(FIRST, len(CHUNKS)):
        part = pieces[4 * (j - FIRST) : 4 * (j - FIRST) + 4]
        near_ref[:, BEGINS[j] : BEGINS[j] + CHUNKS[j]] = total_of(part, x_lo, 1)
        give_ref[:, BEGINS[j] - start : BEGINS[j] - start + CHUNKS[j]] = total_of(part, 1 - x_lo, 1)


def last_sums(kernel, widths, where, keep, got, pieces):
    return pl.pallas_call(
        kernel,
        out_shape=[jax.ShapeDtypeStruct((96, wide), jnp.float32) for wide in widths],
        in_specs=vmem_specs(2 + len(pieces)),
        out_specs=[pl.BlockSpec(memory_space=pltpu.VMEM)] * len(widths),
        cost_estimate=pl.CostEstimate(flops=2 * 3 * 96 * 768, bytes_accessed=4 * 3 * 96 * 768 * 4, transcendentals=0),
        compiler_params=pltpu.CompilerParams(vmem_limit_bytes=VMEM_LIMIT),
    )(where, keep, got, *pieces)


def tied(*values):
    return lax.optimization_barrier(values)


def shards(grad, old_stats):
    rows = grad.shape[0]
    core = lax.axis_index("fsdp") & 1
    y, x_lo = lax.axis_index("tensor") >> 1, lax.axis_index("tensor") & 1
    ahead = core * ((lax.axis_index("fsdp") & 6) == 0)
    where = jnp.stack([core, y, x_lo, ahead]).astype(jnp.int32)

    def spread(pieces):
        return [moved(pieces[hop], along_y(hop)) for hop in (1, 3, 2)]

    def pick(j, span=(0, grad.shape[1])):
        return picked(where, grad, BEGINS[j], CHUNKS[j], span)

    def cross(j):
        return list(crossed(where, here, partner, flight[j], BEGINS[j]))

    partner = moved(grad, swap_cores)
    flight = [moved(pick(0), block_flow)]
    here = held(grad)
    square = squared(where, here)
    *square, partner, out1 = tied(*square, partner, pick(1))
    flight.append(moved(out1, block_flow))
    square_got = spread(square)
    partner = held(partner)
    out2, out3 = pick(2), pick(3)
    flight[0], partner, out2, out3 = tied(flight[0], partner, out2, out3)

    part0 = cross(0)
    *part0, out2, square_got[0], square_got[1], square_got[2] = tied(*part0, out2, *square_got)
    got0 = spread(part0)
    flight.append(moved(out2, block_flow))

    out3, got0[0], got0[1], got0[2] = tied(out3, *got0)
    flight.append(moved(out3, block_flow))
    flight[1], part0[0] = tied(flight[1], part0[0])
    part1 = cross(1)
    got1 = spread(part1)

    flight[2], part1[0] = tied(flight[2], part1[0])
    part2 = cross(2)
    *part2, got1[0], got1[1], got1[2] = tied(*part2, *got1)
    got2 = spread(part2)

    firsts = [square[0], *square_got, part0[0], *got0, part1[0], *got1]
    keep, give = first_sums(where, firsts)
    wide, start = CHUNKS[3], BEGINS[3]
    flops = 2 * rows * wide * grad.shape[1]
    tall = (rows, wide)
    (early,) = product_call(functools.partial(early_kernel, start, wide), [tall], [], flops, where, here, partner)
    flight[3], early, keep = tied(flight[3], early, keep)
    far3, near3 = product_call(middle_kernel, [tall, tall], [], flops, where, here, partner, flight[3])
    give, far3, got2[0], got2[1], got2[2] = tied(give, far3, *got2)
    got = moved(give, swap_x)
    scratch = [tall, (wide, rows), tall]
    part3 = product_call(
        late_kernel, [(2, 2, rows // 8, wide)] * 4, scratch, flops, where, here, partner, flight[3], early, far3, near3
    )
    pieces = [part2[0], *got2, part3[0], *spread(part3)]
    more = rows - BEGINS[FIRST]
    diagonal, near, near_give = last_sums(near_sums_kernel, (rows, rows, more), where, keep, got, pieces)
    far, far_give = last_sums(far_sums_kernel, (rows, more), where, keep, got, pieces)

    near_more = moved(near_give, swap_x)
    far_more = moved(far_give, to_owner_x)
    far = moved(far, to_owner)
    near = near + jnp.pad(near_more, ((0, 0), (rows - more, 0)))
    far_low = jnp.pad(far_more, ((0, 0), (rows - more, 0)))
    turned = [
        far_more[:, BEGINS[j] - BEGINS[FIRST] :][:, :wide].reshape(rows // wide, wide // 8, wide).transpose(1, 0, 2).reshape(wide // 8, rows)
        for j, wide in enumerate(CHUNKS)
        if j >= FIRST
    ]
    far_high = jnp.pad(jnp.concatenate(turned, axis=0), ((96 - more // 8, 0), (0, 0)))
    far = far + jnp.where(core == 0, far_low, far_high)
    summed = jnp.stack([diagonal, near, far], axis=1)
    return decay_rate * old_stats + (1.0 - decay_rate) * COLS ** (-0.5) * summed


def solution(mesh):
    return jax.shard_map(
        shards,
        mesh=mesh,
        in_specs=(P("fsdp", "tensor"), P(("fsdp", "tensor"), None, None)),
        out_specs=P(("fsdp", "tensor"), None, None),
        check_vma=False,
    )
```

```python
import functools

import jax
import jax.numpy as jnp
from jax import lax
from jax.experimental import pallas as pl
from jax.experimental.pallas import tpu as pltpu
from jax.sharding import PartitionSpec as P

COLS = 53248
decay_rate = 0.95
CHUNKS = (256, 256, 128, 128)
BEGINS = (0, 256, 512, 640)
VMEM_LIMIT = 5 << 20
FIRST = 2
AXES = ("fsdp", "tensor")


def place(x_hi, z, core, y, x_lo):
    return ((x_hi % 2) * 8 + (z % 4) * 2 + core) * 8 + (y % 4) * 2 + x_lo


def moved(value, target):
    pairs = []
    for source in range(128):
        block, shard = divmod(source, 8)
        pairs.append((source, target(block // 8, (block // 2) % 4, block % 2, shard // 2, shard % 2)))
    return lax.ppermute(value, AXES, pairs)


def next_chip(x_hi, z, core, y, x_lo, steps):
    chip = (x_hi * 4 + z + steps) % 8
    return place(chip // 4, chip % 4, core, y, x_lo)


def block_flow(x_hi, z, core, y, x_lo):
    return next_chip(x_hi, z, 1 - core, y, x_lo, 1 if core else -1)


def swap_cores(x_hi, z, core, y, x_lo):
    return place(x_hi, z, 1 - core, y, x_lo)


def swap_x(x_hi, z, core, y, x_lo):
    return place(x_hi, z, core, y, 1 - x_lo)


def to_owner(x_hi, z, core, y, x_lo):
    return next_chip(x_hi, z, 1 - core, y, x_lo, 0 if core else -1)


def to_owner_x(x_hi, z, core, y, x_lo):
    return to_owner(x_hi, z, core, y, 1 - x_lo)


def along_y(steps):
    return lambda x_hi, z, core, y, x_lo: place(x_hi, z, core, y + steps, x_lo)


def contract(left, right):
    return lax.dot_general(left, right, (((1,), (1,)), ((), ())), preferred_element_type=jnp.float32)


def pick_kernel(begin, thin, span, grad_ref, out_ref, sems):
    core, y, _, _ = position()
    copies = []
    for i in range(8):
        offset = pl.multiple_of(jnp.where(core == 0, begin + thin * i, 96 * i + begin // 8), 16)
        source = grad_ref.at[pl.ds(offset, thin), pl.ds(span[0], span[1] - span[0])]
        copies.append(pltpu.make_async_copy(source, out_ref.at[pl.ds(thin * i, thin)], sems.at[i]))
    for copy in copies:
        copy.start()
    for copy in copies:
        copy.wait()


def picked(grad, begin, wide, span):
    depth = span[1] - span[0]
    return pl.pallas_call(
        functools.partial(pick_kernel, begin, wide // 8, span),
        out_shape=jax.ShapeDtypeStruct((wide, depth), grad.dtype),
        in_specs=[pl.BlockSpec(memory_space=pl.ANY)],
        out_specs=pl.BlockSpec(memory_space=pltpu.VMEM),
        scratch_shapes=[pltpu.SemaphoreType.DMA((8,))],
        cost_estimate=pl.CostEstimate(flops=0, bytes_accessed=4 * wide * depth, transcendentals=0),
        compiler_params=pltpu.CompilerParams(vmem_limit_bytes=VMEM_LIMIT),
    )(pltpu.with_memory_space_constraint(grad, pltpu.HBM))


def hold_kernel(source_ref, out_ref, sem):
    copy = pltpu.make_async_copy(source_ref, out_ref, sem)
    copy.start()
    copy.wait()


def held(value):
    return pl.pallas_call(
        hold_kernel,
        out_shape=pltpu.VMEM(value.shape, value.dtype),
        in_specs=[pl.BlockSpec(memory_space=pl.ANY)],
        out_specs=pl.BlockSpec(memory_space=pltpu.VMEM),
        scratch_shapes=[pltpu.SemaphoreType.DMA],
        cost_estimate=pl.CostEstimate(flops=0, bytes_accessed=4 * value.size, transcendentals=0),
        compiler_params=pltpu.CompilerParams(vmem_limit_bytes=VMEM_LIMIT),
    )(pltpu.with_memory_space_constraint(value, pltpu.HBM))


def resident(value):
    return pltpu.with_memory_space_constraint(value, pltpu.VMEM)


def vmem_specs(count):
    return [pl.BlockSpec(memory_space=pltpu.VMEM)] * count


def position():
    block, shard = lax.axis_index("fsdp"), lax.axis_index("tensor")
    return block & 1, shard >> 1, shard & 1, (block & 7) == 1


def owner_rows(y, hop, side, count):
    shard = 2 * ((y + hop) & 3) + side
    return pl.ds(pl.multiple_of(count * shard, count), count)


def square_kernel(own_ref, *refs):
    outs, total = refs[:4], refs[4]
    _, y, _, _ = position()
    total[...] = contract(own_ref[...], own_ref[...])
    for hop in range(4):
        for side in range(2):
            outs[hop][side] = total[owner_rows(y, hop, side, 96), :]


def squared(grad):
    rows, depth = grad.shape
    piece = (2, rows // 8, rows)
    return pl.pallas_call(
        square_kernel,
        out_shape=[jax.ShapeDtypeStruct(piece, jnp.float32)] * 4,
        in_specs=vmem_specs(1),
        out_specs=[pl.BlockSpec(memory_space=pltpu.VMEM)] * 4,
        scratch_shapes=[pltpu.VMEM((rows, rows), jnp.float32)],
        cost_estimate=pl.CostEstimate(
            flops=2 * rows * rows * depth, bytes_accessed=2 * depth * rows + 4 * rows * rows, transcendentals=0
        ),
        compiler_params=pltpu.CompilerParams(vmem_limit_bytes=VMEM_LIMIT),
    )(resident(grad))


def cut_up(core, y, tall, flat, mixed, outs):
    wide = mixed.shape[1]
    thin = wide // 8

    @pl.when(core != 0)
    def _():
        for hop in range(4):
            for side in range(2):
                outs[hop][side, 0] = tall[owner_rows(y, hop, side, 96), :]

    @pl.when(core == 0)
    def _():
        for hop in range(4):
            for side in range(2):
                rows = owner_rows(y, hop, side, thin)
                for i in range(768 // wide):
                    outs[hop][side, 0, i * thin : (i + 1) * thin, :] = flat[rows, i * wide : (i + 1) * wide]

    for hop in range(4):
        for side in range(2):
            outs[hop][side, 1] = mixed[owner_rows(y, hop, side, 96), :]


def cross_kernel(begin, own_ref, pair_ref, got_ref, *refs):
    outs, (tall, flat, mixed) = refs[:4], refs[4:]
    core, y, _, _ = position()
    wide = got_ref.shape[0]

    @pl.when(core == 0)
    def _():
        flat[...] = contract(got_ref[...], pair_ref[...])
        mixed[...] = contract(own_ref[...], pair_ref[begin : begin + wide, :])

    @pl.when(core != 0)
    def _():
        tall[...] = contract(pair_ref[...], got_ref[...])
        mixed[...] = contract(own_ref[...], got_ref[...])

    cut_up(core, y, tall, flat, mixed, outs)


def early_kernel(begin, wide, own_ref, pair_ref, mixed_ref):
    @pl.when(position()[0] == 0)
    def _():
        mixed_ref[...] = contract(own_ref[...], pair_ref[begin : begin + wide, :])


def middle_kernel(own_ref, pair_ref, got_ref, tall_ref, mixed_ref):
    @pl.when(position()[3])
    def _():
        tall_ref[...] = contract(pair_ref[...], got_ref[...])
        mixed_ref[...] = contract(own_ref[...], got_ref[...])


def late_kernel(own_ref, pair_ref, got_ref, early_ref, tall_ref, middle_ref, *refs):
    outs, (tall, flat, mixed) = refs[:4], refs[4:]
    core, y, _, ahead = position()

    @pl.when(core == 0)
    def _():
        flat[...] = contract(got_ref[...], pair_ref[...])
        mixed[...] = early_ref[...]

    @pl.when((core != 0) & ~ahead)
    def _():
        tall[...] = contract(pair_ref[...], got_ref[...])
        mixed[...] = contract(own_ref[...], got_ref[...])

    @pl.when(ahead)
    def _():
        tall[...] = tall_ref[...]
        mixed[...] = middle_ref[...]

    cut_up(core, y, tall, flat, mixed, outs)


def product_call(kernel, shapes, scratch, flops, *arrays):
    return pl.pallas_call(
        kernel,
        out_shape=[jax.ShapeDtypeStruct(shape, jnp.float32) for shape in shapes],
        in_specs=vmem_specs(len(arrays)),
        out_specs=[pl.BlockSpec(memory_space=pltpu.VMEM)] * len(shapes),
        scratch_shapes=[pltpu.VMEM(shape, jnp.float32) for shape in scratch],
        cost_estimate=pl.CostEstimate(flops=flops, bytes_accessed=4 * flops // 768, transcendentals=0),
        compiler_params=pltpu.CompilerParams(vmem_limit_bytes=VMEM_LIMIT),
    )(*[resident(array) for array in arrays])


def crossed(grad, partner, arrived, begin):
    wide, depth = arrived.shape
    rows = grad.shape[0]
    pieces = [(2, 2, rows // 8, wide)] * 4
    sums = [(rows, wide), (wide, rows), (rows, wide)]
    kernel = functools.partial(cross_kernel, begin)
    return product_call(kernel, pieces, sums, 4 * rows * wide * depth, grad, partner, arrived)


def total_of(refs, *at):
    return (refs[0][at] + refs[1][at]) + (refs[2][at] + refs[3][at])


def columns_of(product, part):
    start = 768 + product * BEGINS[FIRST] + BEGINS[part]
    return slice(start, start + CHUNKS[part])


def first_sums_kernel(*refs):
    _, _, x_lo, _ = position()
    for side, out_ref in ((x_lo, refs[-2]), (1 - x_lo, refs[-1])):
        out_ref[:, :768] = total_of(refs[:4], side)
        for j in range(FIRST):
            for product in range(2):
                out_ref[:, columns_of(product, j)] = total_of(refs[4 + 4 * j : 8 + 4 * j], side, product)


def first_sums(pieces):
    shape = jax.ShapeDtypeStruct((96, 768 + 2 * BEGINS[FIRST]), jnp.float32)
    return pl.pallas_call(
        first_sums_kernel,
        out_shape=[shape, shape],
        in_specs=vmem_specs(len(pieces)),
        out_specs=[pl.BlockSpec(memory_space=pltpu.VMEM)] * 2,
        cost_estimate=pl.CostEstimate(flops=4 * 3 * 96 * 768 * 2, bytes_accessed=10 * 3 * 96 * 768 * 4, transcendentals=0),
        compiler_params=pltpu.CompilerParams(vmem_limit_bytes=2 * VMEM_LIMIT),
    )(*pieces)


def far_sums_kernel(keep_ref, got_ref, *refs):
    pieces, (far_ref, give_ref) = refs[:-2], refs[-2:]
    core, _, x_lo, _ = position()
    start = BEGINS[FIRST]
    for j in range(FIRST, len(CHUNKS)):
        columns = slice(BEGINS[j] - start, BEGINS[j] - start + CHUNKS[j])
        give_ref[:, columns] = total_of(pieces[4 * (j - FIRST) : 4 * (j - FIRST) + 4], 1 - x_lo, 0)

    @pl.when(core != 0)
    def _():
        far_ref[:, :start] = keep_ref[:, 768 : 768 + start] + got_ref[:, 768 : 768 + start]
        for j in range(FIRST, len(CHUNKS)):
            columns = slice(BEGINS[j], BEGINS[j] + CHUNKS[j])
            far_ref[:, columns] = total_of(pieces[4 * (j - FIRST) : 4 * (j - FIRST) + 4], x_lo, 0)

    @pl.when(core == 0)
    def _():
        for j, (begin, wide) in enumerate(zip(BEGINS, CHUNKS)):
            thin = wide // 8
            for i in range(768 // wide):
                rows = slice(i * thin, (i + 1) * thin)
                if j < FIRST:
                    value = keep_ref[rows, columns_of(0, j)] + got_ref[rows, columns_of(0, j)]
                else:
                    value = total_of(pieces[4 * (j - FIRST) : 4 * (j - FIRST) + 4], x_lo, 0, rows)
                far_ref[begin // 8 : begin // 8 + thin, i * wide : (i + 1) * wide] = value


def near_sums_kernel(keep_ref, got_ref, *refs):
    pieces, (diagonal_ref, near_ref, give_ref) = refs[:-3], refs[-3:]
    _, _, x_lo, _ = position()
    start = BEGINS[FIRST]
    diagonal_ref[...] = keep_ref[:, :768] + got_ref[:, :768]
    near_ref[:, :start] = keep_ref[:, 768 + start :] + got_ref[:, 768 + start :]
    for j in range(FIRST, len(CHUNKS)):
        part = pieces[4 * (j - FIRST) : 4 * (j - FIRST) + 4]
        near_ref[:, BEGINS[j] : BEGINS[j] + CHUNKS[j]] = total_of(part, x_lo, 1)
        give_ref[:, BEGINS[j] - start : BEGINS[j] - start + CHUNKS[j]] = total_of(part, 1 - x_lo, 1)


def last_sums_kernel(keep_ref, got_ref, *refs):
    pieces, outs = refs[:-5], refs[-5:]
    far_sums_kernel(keep_ref, got_ref, *pieces, *outs[:2])
    near_sums_kernel(keep_ref, got_ref, *pieces, *outs[2:])


def last_sums(kernel, widths, keep, got, pieces):
    return pl.pallas_call(
        kernel,
        out_shape=[jax.ShapeDtypeStruct((96, wide), jnp.float32) for wide in widths],
        in_specs=vmem_specs(2 + len(pieces)),
        out_specs=[pl.BlockSpec(memory_space=pltpu.VMEM)] * len(widths),
        cost_estimate=pl.CostEstimate(flops=2 * 3 * 96 * 768, bytes_accessed=4 * 3 * 96 * 768 * 4, transcendentals=0),
        compiler_params=pltpu.CompilerParams(vmem_limit_bytes=VMEM_LIMIT),
    )(keep, got, *pieces)


def tied(*values):
    return lax.optimization_barrier(values)


def shards(grad, old_stats):
    rows = grad.shape[0]
    core = position()[0]

    def spread(pieces):
        return [moved(pieces[hop], along_y(hop)) for hop in (1, 3, 2)]

    def pick(j, span=(0, grad.shape[1])):
        return picked(grad, BEGINS[j], CHUNKS[j], span)

    def cross(j):
        return list(crossed(here, partner, flight[j], BEGINS[j]))

    partner = moved(grad, swap_cores)
    flight = [moved(pick(0), block_flow)]
    here = held(grad)
    square = squared(here)
    *square, partner, out1 = tied(*square, partner, pick(1))
    flight.append(moved(out1, block_flow))
    square_got = spread(square)
    partner = held(partner)
    out2, out3 = pick(2), pick(3)
    flight[0], partner, out2, out3 = tied(flight[0], partner, out2, out3)

    part0 = cross(0)
    *part0, out2, square_got[0], square_got[1], square_got[2] = tied(*part0, out2, *square_got)
    got0 = spread(part0)
    flight.append(moved(out2, block_flow))

    out3, got0[0], got0[1], got0[2] = tied(out3, *got0)
    flight.append(moved(out3, block_flow))
    flight[1], part0[0] = tied(flight[1], part0[0])
    part1 = cross(1)
    got1 = spread(part1)

    flight[2], part1[0] = tied(flight[2], part1[0])
    part2 = cross(2)
    *part2, got1[0], got1[1], got1[2] = tied(*part2, *got1)
    got2 = spread(part2)

    firsts = [square[0], *square_got, part0[0], *got0, part1[0], *got1]
    keep, give = first_sums(firsts)
    wide, start = CHUNKS[3], BEGINS[3]
    flops = 2 * rows * wide * grad.shape[1]
    tall = (rows, wide)
    (early,) = product_call(functools.partial(early_kernel, start, wide), [tall], [], flops, here, partner)
    flight[3], early, keep = tied(flight[3], early, keep)
    far3, near3 = product_call(middle_kernel, [tall, tall], [], flops, here, partner, flight[3])
    give, far3, got2[0], got2[1], got2[2] = tied(give, far3, *got2)
    got = moved(give, swap_x)
    scratch = [tall, (wide, rows), tall]
    part3 = product_call(
        late_kernel, [(2, 2, rows // 8, wide)] * 4, scratch, flops, here, partner, flight[3], early, far3, near3
    )
    pieces = [part2[0], *got2, part3[0], *spread(part3)]
    more = rows - BEGINS[FIRST]
    widths = (rows, more, rows, rows, more)
    far, far_give, diagonal, near, near_give = last_sums(last_sums_kernel, widths, keep, got, pieces)

    near_more = moved(near_give, swap_x)
    far_more = moved(far_give, to_owner_x)
    far = moved(far, to_owner)
    near = near + jnp.pad(near_more, ((0, 0), (rows - more, 0)))
    far_low = jnp.pad(far_more, ((0, 0), (rows - more, 0)))
    turned = [
        far_more[:, BEGINS[j] - BEGINS[FIRST] :][:, :wide].reshape(rows // wide, wide // 8, wide).transpose(1, 0, 2).reshape(wide // 8, rows)
        for j, wide in enumerate(CHUNKS)
        if j >= FIRST
    ]
    far_high = jnp.pad(jnp.concatenate(turned, axis=0), ((96 - more // 8, 0), (0, 0)))
    far = jnp.where(core == 0, far_low, far_high) + far
    summed = jnp.stack([diagonal, near, far], axis=1)
    return decay_rate * old_stats + (1.0 - decay_rate) * COLS ** (-0.5) * summed


def solution(mesh):
    return jax.shard_map(
        shards,
        mesh=mesh,
        in_specs=(P("fsdp", "tensor"), P(("fsdp", "tensor"), None, None)),
        out_specs=P(("fsdp", "tensor"), None, None),
        check_vma=False,
    )
```

```python
import functools

import jax
import jax.numpy as jnp
from jax import lax
from jax.experimental import pallas as pl
from jax.experimental.pallas import tpu as pltpu
from jax.sharding import PartitionSpec as P

COLS = 53248
decay_rate = 0.95
CHUNKS = (256, 256, 128, 128)
BEGINS = (0, 256, 512, 640)
VMEM_LIMIT = 5 << 20
FIRST = 2
AXES = ("fsdp", "tensor")


def place(x_hi, z, core, y, x_lo):
    return ((x_hi % 2) * 8 + (z % 4) * 2 + core) * 8 + (y % 4) * 2 + x_lo


def moved(value, target):
    pairs = []
    for source in range(128):
        block, shard = divmod(source, 8)
        pairs.append((source, target(block // 8, (block // 2) % 4, block % 2, shard // 2, shard % 2)))
    return lax.ppermute(value, AXES, pairs)


def next_chip(x_hi, z, core, y, x_lo, steps):
    chip = (x_hi * 4 + z + steps) % 8
    return place(chip // 4, chip % 4, core, y, x_lo)


def block_flow(x_hi, z, core, y, x_lo):
    return next_chip(x_hi, z, 1 - core, y, x_lo, 1 if core else -1)


def swap_cores(x_hi, z, core, y, x_lo):
    return place(x_hi, z, 1 - core, y, x_lo)


def swap_x(x_hi, z, core, y, x_lo):
    return place(x_hi, z, core, y, 1 - x_lo)


def to_owner(x_hi, z, core, y, x_lo):
    return next_chip(x_hi, z, 1 - core, y, x_lo, 0 if core else -1)


def to_owner_x(x_hi, z, core, y, x_lo):
    return to_owner(x_hi, z, core, y, 1 - x_lo)


def along_y(steps):
    return lambda x_hi, z, core, y, x_lo: place(x_hi, z, core, y + steps, x_lo)


def contract(left, right):
    return lax.dot_general(left, right, (((1,), (1,)), ((), ())), preferred_element_type=jnp.float32)


def pick_kernel(begin, thin, span, grad_ref, out_ref, sems):
    core, y, _, _ = position()
    copies = []
    for i in range(8):
        offset = pl.multiple_of(jnp.where(core == 0, begin + thin * i, 96 * i + begin // 8), 16)
        source = grad_ref.at[pl.ds(offset, thin), pl.ds(span[0], span[1] - span[0])]
        copies.append(pltpu.make_async_copy(source, out_ref.at[pl.ds(thin * i, thin)], sems.at[i]))
    for copy in copies:
        copy.start()
    for copy in copies:
        copy.wait()


def picked(grad, begin, wide, span):
    depth = span[1] - span[0]
    return pl.pallas_call(
        functools.partial(pick_kernel, begin, wide // 8, span),
        out_shape=jax.ShapeDtypeStruct((wide, depth), grad.dtype),
        in_specs=[pl.BlockSpec(memory_space=pl.ANY)],
        out_specs=pl.BlockSpec(memory_space=pltpu.VMEM),
        scratch_shapes=[pltpu.SemaphoreType.DMA((8,))],
        cost_estimate=pl.CostEstimate(flops=0, bytes_accessed=4 * wide * depth, transcendentals=0),
        compiler_params=pltpu.CompilerParams(vmem_limit_bytes=VMEM_LIMIT),
    )(pltpu.with_memory_space_constraint(grad, pltpu.HBM))


def hold_kernel(source_ref, out_ref, sem):
    copy = pltpu.make_async_copy(source_ref, out_ref, sem)
    copy.start()
    copy.wait()


def held(value):
    return pl.pallas_call(
        hold_kernel,
        out_shape=pltpu.VMEM(value.shape, value.dtype),
        in_specs=[pl.BlockSpec(memory_space=pl.ANY)],
        out_specs=pl.BlockSpec(memory_space=pltpu.VMEM),
        scratch_shapes=[pltpu.SemaphoreType.DMA],
        cost_estimate=pl.CostEstimate(flops=0, bytes_accessed=4 * value.size, transcendentals=0),
        compiler_params=pltpu.CompilerParams(vmem_limit_bytes=VMEM_LIMIT),
    )(pltpu.with_memory_space_constraint(value, pltpu.HBM))


def resident(value):
    return pltpu.with_memory_space_constraint(value, pltpu.VMEM)


def vmem_specs(count):
    return [pl.BlockSpec(memory_space=pltpu.VMEM)] * count


def position():
    block, shard = lax.axis_index("fsdp"), lax.axis_index("tensor")
    return block & 1, shard >> 1, shard & 1, (block & 7) == 1


def owner_rows(y, hop, side, count):
    shard = 2 * ((y + hop) & 3) + side
    return pl.ds(pl.multiple_of(count * shard, count), count)


def square_kernel(own_ref, *refs):
    outs, total = refs[:4], refs[4]
    _, y, _, _ = position()
    total[...] = contract(own_ref[...], own_ref[...])
    for hop in range(4):
        for side in range(2):
            outs[hop][side] = total[owner_rows(y, hop, side, 96), :]


def squared(grad):
    rows, depth = grad.shape
    piece = (2, rows // 8, rows)
    return pl.pallas_call(
        square_kernel,
        out_shape=[jax.ShapeDtypeStruct(piece, jnp.float32)] * 4,
        in_specs=vmem_specs(1),
        out_specs=[pl.BlockSpec(memory_space=pltpu.VMEM)] * 4,
        scratch_shapes=[pltpu.VMEM((rows, rows), jnp.float32)],
        cost_estimate=pl.CostEstimate(
            flops=2 * rows * rows * depth, bytes_accessed=2 * depth * rows + 4 * rows * rows, transcendentals=0
        ),
        compiler_params=pltpu.CompilerParams(vmem_limit_bytes=VMEM_LIMIT),
    )(resident(grad))


def cut_up(core, y, tall, flat, mixed, outs):
    wide = mixed.shape[1]
    thin = wide // 8

    @pl.when(core != 0)
    def _():
        for hop in range(4):
            for side in range(2):
                outs[hop][side, 0] = tall[owner_rows(y, hop, side, 96), :]

    @pl.when(core == 0)
    def _():
        for hop in range(4):
            for side in range(2):
                rows = owner_rows(y, hop, side, thin)
                for i in range(768 // wide):
                    outs[hop][side, 0, i * thin : (i + 1) * thin, :] = flat[rows, i * wide : (i + 1) * wide]

    for hop in range(4):
        for side in range(2):
            outs[hop][side, 1] = mixed[owner_rows(y, hop, side, 96), :]


def cross_kernel(begin, own_ref, pair_ref, got_ref, *refs):
    outs, (tall, flat, mixed) = refs[:4], refs[4:]
    core, y, _, _ = position()
    wide = got_ref.shape[0]

    @pl.when(core == 0)
    def _():
        flat[...] = contract(got_ref[...], pair_ref[...])
        mixed[...] = contract(own_ref[...], pair_ref[begin : begin + wide, :])

    @pl.when(core != 0)
    def _():
        tall[...] = contract(pair_ref[...], got_ref[...])
        mixed[...] = contract(own_ref[...], got_ref[...])

    cut_up(core, y, tall, flat, mixed, outs)


def early_kernel(begin, wide, own_ref, pair_ref, mixed_ref):
    @pl.when(position()[0] == 0)
    def _():
        mixed_ref[...] = contract(own_ref[...], pair_ref[begin : begin + wide, :])


def middle_kernel(own_ref, pair_ref, got_ref, tall_ref, mixed_ref):
    @pl.when(position()[3])
    def _():
        tall_ref[...] = contract(pair_ref[...], got_ref[...])
        mixed_ref[...] = contract(own_ref[...], got_ref[...])


def late_kernel(own_ref, pair_ref, got_ref, early_ref, tall_ref, middle_ref, *refs):
    outs, (tall, flat, mixed) = refs[:4], refs[4:]
    core, y, _, ahead = position()

    @pl.when(core == 0)
    def _():
        flat[...] = contract(got_ref[...], pair_ref[...])
        cut_up(core, y, tall, flat, early_ref, outs)

    @pl.when((core != 0) & ~ahead)
    def _():
        tall[...] = contract(pair_ref[...], got_ref[...])
        mixed[...] = contract(own_ref[...], got_ref[...])
        cut_up(core, y, tall, flat, mixed, outs)

    @pl.when(ahead)
    def _():
        cut_up(core, y, tall_ref, flat, middle_ref, outs)


def product_call(kernel, shapes, scratch, flops, *arrays):
    return pl.pallas_call(
        kernel,
        out_shape=[jax.ShapeDtypeStruct(shape, jnp.float32) for shape in shapes],
        in_specs=vmem_specs(len(arrays)),
        out_specs=[pl.BlockSpec(memory_space=pltpu.VMEM)] * len(shapes),
        scratch_shapes=[pltpu.VMEM(shape, jnp.float32) for shape in scratch],
        cost_estimate=pl.CostEstimate(flops=flops, bytes_accessed=4 * flops // 768, transcendentals=0),
        compiler_params=pltpu.CompilerParams(vmem_limit_bytes=VMEM_LIMIT),
    )(*[resident(array) for array in arrays])


def crossed(grad, partner, arrived, begin):
    wide, depth = arrived.shape
    rows = grad.shape[0]
    pieces = [(2, 2, rows // 8, wide)] * 4
    sums = [(rows, wide), (wide, rows), (rows, wide)]
    kernel = functools.partial(cross_kernel, begin)
    return product_call(kernel, pieces, sums, 4 * rows * wide * depth, grad, partner, arrived)


def total_of(refs, *at):
    return (refs[0][at] + refs[1][at]) + (refs[2][at] + refs[3][at])


def columns_of(product, part):
    start = 768 + product * BEGINS[FIRST] + BEGINS[part]
    return slice(start, start + CHUNKS[part])


def first_sums_kernel(*refs):
    _, _, x_lo, _ = position()
    for side, out_ref in ((x_lo, refs[-2]), (1 - x_lo, refs[-1])):
        out_ref[:, :768] = total_of(refs[:4], side)
        for j in range(FIRST):
            for product in range(2):
                out_ref[:, columns_of(product, j)] = total_of(refs[4 + 4 * j : 8 + 4 * j], side, product)


def first_sums(pieces):
    shape = jax.ShapeDtypeStruct((96, 768 + 2 * BEGINS[FIRST]), jnp.float32)
    return pl.pallas_call(
        first_sums_kernel,
        out_shape=[shape, shape],
        in_specs=vmem_specs(len(pieces)),
        out_specs=[pl.BlockSpec(memory_space=pltpu.VMEM)] * 2,
        cost_estimate=pl.CostEstimate(flops=4 * 3 * 96 * 768 * 2, bytes_accessed=10 * 3 * 96 * 768 * 4, transcendentals=0),
        compiler_params=pltpu.CompilerParams(vmem_limit_bytes=2 * VMEM_LIMIT),
    )(*pieces)


def far_sums_kernel(keep_ref, got_ref, *refs):
    pieces, (far_ref, give_ref) = refs[:-2], refs[-2:]
    core, _, x_lo, _ = position()
    start = BEGINS[FIRST]
    for j in range(FIRST, len(CHUNKS)):
        columns = slice(BEGINS[j] - start, BEGINS[j] - start + CHUNKS[j])
        give_ref[:, columns] = total_of(pieces[4 * (j - FIRST) : 4 * (j - FIRST) + 4], 1 - x_lo, 0)

    @pl.when(core != 0)
    def _():
        far_ref[:, :start] = keep_ref[:, 768 : 768 + start] + got_ref[:, 768 : 768 + start]
        for j in range(FIRST, len(CHUNKS)):
            columns = slice(BEGINS[j], BEGINS[j] + CHUNKS[j])
            far_ref[:, columns] = total_of(pieces[4 * (j - FIRST) : 4 * (j - FIRST) + 4], x_lo, 0)

    @pl.when(core == 0)
    def _():
        for j, (begin, wide) in enumerate(zip(BEGINS, CHUNKS)):
            thin = wide // 8
            for i in range(768 // wide):
                rows = slice(i * thin, (i + 1) * thin)
                if j < FIRST:
                    value = keep_ref[rows, columns_of(0, j)] + got_ref[rows, columns_of(0, j)]
                else:
                    value = total_of(pieces[4 * (j - FIRST) : 4 * (j - FIRST) + 4], x_lo, 0, rows)
                far_ref[begin // 8 : begin // 8 + thin, i * wide : (i + 1) * wide] = value


def near_sums_kernel(keep_ref, got_ref, *refs):
    pieces, (diagonal_ref, near_ref, give_ref) = refs[:-3], refs[-3:]
    _, _, x_lo, _ = position()
    start = BEGINS[FIRST]
    diagonal_ref[...] = keep_ref[:, :768] + got_ref[:, :768]
    near_ref[:, :start] = keep_ref[:, 768 + start :] + got_ref[:, 768 + start :]
    for j in range(FIRST, len(CHUNKS)):
        part = pieces[4 * (j - FIRST) : 4 * (j - FIRST) + 4]
        near_ref[:, BEGINS[j] : BEGINS[j] + CHUNKS[j]] = total_of(part, x_lo, 1)
        give_ref[:, BEGINS[j] - start : BEGINS[j] - start + CHUNKS[j]] = total_of(part, 1 - x_lo, 1)


def last_sums_kernel(keep_ref, got_ref, *refs):
    pieces, outs = refs[:-5], refs[-5:]
    far_sums_kernel(keep_ref, got_ref, *pieces, *outs[:2])
    near_sums_kernel(keep_ref, got_ref, *pieces, *outs[2:])


def last_sums(kernel, widths, keep, got, pieces):
    return pl.pallas_call(
        kernel,
        out_shape=[jax.ShapeDtypeStruct((96, wide), jnp.float32) for wide in widths],
        in_specs=vmem_specs(2 + len(pieces)),
        out_specs=[pl.BlockSpec(memory_space=pltpu.VMEM)] * len(widths),
        cost_estimate=pl.CostEstimate(flops=2 * 3 * 96 * 768, bytes_accessed=4 * 3 * 96 * 768 * 4, transcendentals=0),
        compiler_params=pltpu.CompilerParams(vmem_limit_bytes=VMEM_LIMIT),
    )(keep, got, *pieces)


def tied(*values):
    return lax.optimization_barrier(values)


def shards(grad, old_stats):
    rows = grad.shape[0]
    core = position()[0]

    def spread(pieces):
        return [moved(pieces[hop], along_y(hop)) for hop in (1, 3, 2)]

    def pick(j, span=(0, grad.shape[1])):
        return picked(grad, BEGINS[j], CHUNKS[j], span)

    def cross(j):
        return list(crossed(here, partner, flight[j], BEGINS[j]))

    partner = moved(grad, swap_cores)
    flight = [moved(pick(0), block_flow)]
    here = held(grad)
    square = squared(here)
    *square, partner, out1 = tied(*square, partner, pick(1))
    flight.append(moved(out1, block_flow))
    square_got = spread(square)
    partner = held(partner)
    out2, out3 = pick(2), pick(3)
    flight[0], partner, out2, out3 = tied(flight[0], partner, out2, out3)

    part0 = cross(0)
    *part0, out2, square_got[0], square_got[1], square_got[2] = tied(*part0, out2, *square_got)
    got0 = spread(part0)
    flight.append(moved(out2, block_flow))

    out3, got0[0], got0[1], got0[2] = tied(out3, *got0)
    flight.append(moved(out3, block_flow))
    flight[1], part0[0] = tied(flight[1], part0[0])
    part1 = cross(1)
    got1 = spread(part1)

    flight[2], part1[0] = tied(flight[2], part1[0])
    part2 = cross(2)
    *part2, got1[0], got1[1], got1[2] = tied(*part2, *got1)
    got2 = spread(part2)

    firsts = [square[0], *square_got, part0[0], *got0, part1[0], *got1]
    keep, give = first_sums(firsts)
    wide, start = CHUNKS[3], BEGINS[3]
    flops = 2 * rows * wide * grad.shape[1]
    tall = (rows, wide)
    (early,) = product_call(functools.partial(early_kernel, start, wide), [tall], [], flops, here, partner)
    flight[3], early, keep = tied(flight[3], early, keep)
    far3, near3 = product_call(middle_kernel, [tall, tall], [], flops, here, partner, flight[3])
    give, far3, got2[0], got2[1], got2[2] = tied(give, far3, *got2)
    got = moved(give, swap_x)
    scratch = [tall, (wide, rows), tall]
    part3 = product_call(
        late_kernel, [(2, 2, rows // 8, wide)] * 4, scratch, flops, here, partner, flight[3], early, far3, near3
    )
    pieces = [part2[0], *got2, part3[0], *spread(part3)]
    more = rows - BEGINS[FIRST]
    widths = (rows, more, rows, rows, more)
    far, far_give, diagonal, near, near_give = last_sums(last_sums_kernel, widths, keep, got, pieces)

    near_more = moved(near_give, swap_x)
    far_more = moved(far_give, to_owner_x)
    far = moved(far, to_owner)
    near = near + jnp.pad(near_more, ((0, 0), (rows - more, 0)))
    far_low = jnp.pad(far_more, ((0, 0), (rows - more, 0)))
    turned = [
        far_more[:, BEGINS[j] - BEGINS[FIRST] :][:, :wide].reshape(rows // wide, wide // 8, wide).transpose(1, 0, 2).reshape(wide // 8, rows)
        for j, wide in enumerate(CHUNKS)
        if j >= FIRST
    ]
    far_high = jnp.pad(jnp.concatenate(turned, axis=0), ((96 - more // 8, 0), (0, 0)))
    far = jnp.where(core == 0, far_low, far_high) + far
    summed = jnp.stack([diagonal, near, far], axis=1)
    return decay_rate * old_stats + (1.0 - decay_rate) * COLS ** (-0.5) * summed


def solution(mesh):
    return jax.shard_map(
        shards,
        mesh=mesh,
        in_specs=(P("fsdp", "tensor"), P(("fsdp", "tensor"), None, None)),
        out_specs=P(("fsdp", "tensor"), None, None),
        check_vma=False,
    )
```
